32 devices in a mesh: group: 2 (over x), expert: 16 (over z, y, core).
Axes of the slice: x: 2, y: 2, z: 4, core: 2. Of those that a mesh axis runs over, the one named last changes fastest.
Arguments:
- tokens: bfloat16 [128, 7168], P(('group', 'expert')), parts along dimension 0, may hold values from -6 to 6
- expert_ids: int32 [128, 2], P(('group', 'expert')), parts along dimension 0, may hold values from 0 to 1, all different within a row; in each aligned block of 4 rows (0 to 3, 4 to 7, ...) at most 4 rows name the same one
- gate_codes: int32 [128, 2], P(('group', 'expert')), parts along dimension 0, may hold values from 1 to 65535
- gate_weight: bfloat16 [16, 7168, 256], P('expert'), may hold values from -0.0625 to 0.0625
- up_weight: bfloat16 [16, 7168, 256], P('expert'), may hold values from -0.0625 to 0.0625
- down_weight: bfloat16 [16, 256, 7168], P('expert'), may hold values from -0.125 to 0.125
- target_basis: bfloat16 [7168, 512], P('expert'), may hold values from -0.0625 to 0.0625
Outputs:
- targets: bfloat16 [128, 512], P(('group', 'expert')), parts along dimension 0
The draws below stay inside these ranges and needn't reach their ends.
There are 2 independent parts, one for each index of `group`. The reference program is written for one: setup_inputs(seed, part) draws one part's arguments, and reference() takes and returns one part's arrays. A program takes and returns all parts, laid end to end along the dimension named above; an argument that names none is the same for every part. Nothing has to cross between parts.
Inputs may be any that keep to these rules, and one draw needn't show every extreme that they name: `expert_ids`: each row names 2 different experts; among the 4 rows of one device no expert is named more than 4 times, a bound that some block reaches.
All inputs are finite; a program needn't handle non-finite values.
Results may differ from the reference program's by a relative error of at most 0.0057.
Values may be sent and summed in bfloat16 or wider, within the bound.
A program may use at most 128 MiB of HBM per device.

```python
import math
import jax
import jax.numpy as jnp
import numpy as np
from jax import lax

D = 7168
EH = 2048
R = 512
SLICES = 8
TOK_DEV = 4
EH_PART = 256
EXPERTS = 2
TOPK = 2
TOKENS = 64
CAP = 4
N_EXPERT = 16


def place_ends(drawn, rng, least, largest):
    longest = drawn.shape.index(max(drawn.shape))
    spots = []
    for shift in (0, 1):
        where = [jax.random.randint(jax.random.fold_in(rng, axis), (), 0, length) for axis, length in enumerate(drawn.shape)]
        where[longest] = (where[longest] + shift) % drawn.shape[longest]
        spots.append(tuple(where))
    return drawn.at[spots[0]].set(least).at[spots[1]].set(largest)


def block_levels(rng, dims, cuts, least, top_value):
    gain = 1.0
    for position, blocks in cuts:
        heights = jax.random.uniform(jax.random.fold_in(jax.random.fold_in(rng, 6), position), (blocks,), jnp.float32, least / len(cuts), top_value / len(cuts))
        gain = gain * jnp.repeat(jnp.exp(heights), dims[position] // blocks).reshape((-1,) + (1,) * (len(dims) - 1 - position))
    return gain


def routed_block(key, own, number, rows, amount, top, bound, lean):
    ranking = jax.random.permutation(key, amount)
    crowded, usual = load_shares(amount, rows * top, bound, lean, True), load_shares(amount, rows * top, bound, lean, False)
    places = jnp.arange(amount)

    def named(sizes, rotation):
        used = int((sizes > 0).sum())
        fixed = max(1, used // 4)
        passed = fixed + (places - fixed + rotation * (used - fixed)) % max(1, amount - fixed)
        return jnp.zeros((amount,), jnp.int32).at[ranking[jnp.where(places < fixed, places, passed)]].set(jnp.asarray(sizes, jnp.int32))

    sizes = jnp.where(number % 4 == 0, named(crowded, number // 4), named(usual, number - number // 4 - 1))
    mixed = jax.random.permutation(jax.random.fold_in(own, 3), amount)
    donor, receiver = mixed[0:amount // 2 * 2:2], mixed[1:amount // 2 * 2:2]
    slack = jnp.minimum(sizes[donor] - 1, bound - sizes[receiver]) // 2
    slack = jnp.where((donor == ranking[0]) | (receiver == ranking[0]) | (sizes[receiver] == 0), 0, jnp.maximum(slack, 0))
    passed = jax.random.randint(jax.random.fold_in(own, 4), (amount // 2,), 0, 1 << 20) % (slack + 1)
    sizes = sizes.at[donor].add(-passed).at[receiver].add(passed)
    labels = jnp.searchsorted(jnp.cumsum(sizes), jnp.arange(rows * top), side="right").astype(jnp.int32)
    table = labels.reshape(top, rows).T
    table = table[jax.random.permutation(jax.random.fold_in(own, 1), rows)]
    rotation = jax.random.randint(jax.random.fold_in(own, 2), (rows, 1), 0, top)
    return jnp.take_along_axis(table, (jnp.arange(top)[None, :] + rotation) % top, axis=1)


def load_shares(count, total, limit, slope, full):
    portions = [(1 << 20) // math.isqrt(rank ** slope) + 1 for rank in range(1, count + 1)]
    largest = limit if full else min(limit, max(-(-total // count), total * portions[0] // sum(portions)))
    least = 1 if total - largest >= count - 1 else 0
    given, rest = [largest] + [least] * (count - 1), total - largest - least * (count - 1)
    while rest > 0:
        free = [i for i in range(1, count) if given[i] < largest] or [i for i in range(1, count) if given[i] < limit]
        whole, remaining = sum([portions[i] for i in free]), rest
        for i in free:
            more = min(limit - given[i], max(1, remaining * portions[i] // whole), rest)
            given[i] = given[i] + more
            rest = rest - more
    return np.array(given)


def centred(stream_key, shape, width, bound, pieces=(), kind=jnp.bfloat16):
    factor_of = block_levels(stream_key, shape, pieces, -0.22, 0.18) if pieces else 1.0
    values = jax.random.normal(stream_key, shape, jnp.float32) * width * factor_of
    return jnp.minimum(jnp.maximum(values, -bound), bound).astype(kind)


def setup_inputs(seed: int = 0, part: int = 0) -> dict:
    keys = jax.random.split(jax.random.key(seed), 8)
    part_splits = jax.random.split(jax.random.fold_in(keys[7], part), 8)
    tokens = centred(part_splits[0], (TOKENS, D), 1.0, 6.0, ((0, 16),))
    expert_ids_keys = jax.random.split(jax.random.fold_in(part_splits[1], 1), TOKENS // TOK_DEV)
    expert_ids_turns = jax.random.permutation(jax.random.fold_in(part_splits[1], 3), TOKENS // TOK_DEV)
    expert_ids = jax.vmap(lambda own, number: routed_block(jax.random.fold_in(part_splits[1], 2), own, number, TOK_DEV, EXPERTS, TOPK, CAP, 2))(expert_ids_keys, expert_ids_turns).reshape((TOKENS, TOPK))
    gate_codes = place_ends(jax.random.randint(part_splits[2], (TOKENS, TOPK), 1, 65536), jax.random.fold_in(part_splits[2], 1), 1, 65535).astype(jnp.int32)
    gate_weight = centred(keys[3], (N_EXPERT, D, EH_PART), D ** -0.5, 0.0625, ((0, 16),))
    up_weight = centred(keys[4], (N_EXPERT, D, EH_PART), D ** -0.5, 0.0625, ((0, 16),))
    down_weight = centred(keys[5], (N_EXPERT, EH_PART, D), EH ** -0.5, 0.125, ((0, 16),))
    target_basis = centred(keys[6], (D, R), D ** -0.5, 0.0625, ((0, 16),))
    return dict(tokens=tokens, expert_ids=expert_ids, gate_codes=gate_codes, gate_weight=gate_weight, up_weight=up_weight, down_weight=down_weight, target_basis=target_basis)


def reference(tokens, expert_ids, gate_codes, gate_weight, up_weight, down_weight, target_basis):
    flat_ids = expert_ids.reshape(-1)
    onehot = (flat_ids[:, None] == jnp.arange(EXPERTS, dtype=jnp.int32)[None, :]).astype(jnp.int32)
    before = jnp.cumsum(onehot, axis=0) - onehot
    slot_rank = jnp.sum(before * onehot, axis=1).astype(jnp.int32)
    row_token = (jnp.arange(TOKENS * TOPK, dtype=jnp.int32) // TOPK).astype(jnp.int32)
    slot_table = jnp.full((EXPERTS, N_EXPERT * CAP), TOKENS, jnp.int32).at[flat_ids, slot_rank].set(row_token)
    padded = jnp.concatenate([tokens, jnp.zeros((1, D), tokens.dtype)], axis=0)
    gate_split = gate_weight.reshape(EXPERTS, SLICES, D, EH_PART)
    up_split = up_weight.reshape(EXPERTS, SLICES, D, EH_PART)
    down_split = down_weight.reshape(EXPERTS, SLICES, EH_PART, D)

    def expert_work(inputs):
        expert_table, gate_mats, up_mats, down_mats = inputs
        row_block = padded[expert_table]
        total = jnp.zeros((N_EXPERT * CAP, R), jnp.float32)
        for slice_index in range(SLICES):
            gate_act = jnp.dot(row_block, gate_mats[slice_index], preferred_element_type=jnp.float32)
            up_act = jnp.dot(row_block, up_mats[slice_index], preferred_element_type=jnp.float32)
            hidden = (jax.nn.silu(gate_act) * up_act).astype(jnp.bfloat16)
            expert_part = jnp.dot(hidden, down_mats[slice_index], preferred_element_type=jnp.float32).astype(jnp.bfloat16)
            total = total + jnp.dot(expert_part, target_basis, preferred_element_type=jnp.float32)
        return total

    per_expert = lax.map(expert_work, (slot_table, gate_split, up_split, down_split))
    projected = per_expert[expert_ids, slot_rank.reshape(TOKENS, TOPK)]
    codes_float = gate_codes.astype(jnp.float32)
    weights = 2.5 * codes_float / jnp.sum(codes_float, axis=1, keepdims=True)
    return jnp.sum(weights[:, :, None] * projected, axis=1).astype(jnp.bfloat16)
```

```python
import functools

import jax
import jax.numpy as jnp
from jax import lax
from jax.experimental import pallas as pl
from jax.experimental.pallas import tpu as pltpu
from jax.sharding import PartitionSpec as P

SLICES = 8
LANES = 128
ROWS = 16
MESH = pl.DeviceIdType.MESH


def run_expert(received, gate_weight, up_weight, down_weight):
    sources, slots, feature_width = received.shape
    row_block = received.reshape(sources * slots, feature_width)
    gate_act = jnp.dot(row_block, gate_weight[0], preferred_element_type=jnp.float32)
    up_act = jnp.dot(row_block, up_weight[0], preferred_element_type=jnp.float32)
    hidden = (jax.nn.silu(gate_act) * up_act).astype(jnp.bfloat16)
    expert_part = jnp.dot(hidden, down_weight[0], preferred_element_type=jnp.float32).astype(
        jnp.bfloat16
    )
    return expert_part.reshape(sources, slots, feature_width)


def gathered(tokens, expert_ids, gate_codes, gate_weight, up_weight, down_weight, target_basis):
    token_count, feature_width = tokens.shape
    pick_count = expert_ids.shape[1]
    owner_count = lax.axis_size("expert")
    expert_count = owner_count // SLICES
    capacity = min(token_count, max(2, 5 * token_count * pick_count // (4 * expert_count)))
    rank_width = target_basis.shape[1]
    flat_ids = expert_ids.reshape(-1)
    order = jnp.arange(token_count * pick_count, dtype=jnp.int32)
    same = (flat_ids[:, None] == flat_ids[None, :]) & (order[None, :] < order[:, None])
    slot_rank = jnp.sum(same.astype(jnp.int32), axis=1)
    slot_index = flat_ids * capacity + slot_rank
    row_token = order // pick_count
    slot_table = (
        jnp.full((expert_count * capacity,), token_count, jnp.int32).at[slot_index].set(row_token)
    )
    padded = jnp.concatenate([tokens, jnp.zeros((1, feature_width), tokens.dtype)], axis=0)
    per_expert_rows = padded[slot_table].reshape(expert_count, 1, capacity, feature_width)
    outgoing = jnp.broadcast_to(per_expert_rows, (expert_count, SLICES, capacity, feature_width))
    outgoing = outgoing.reshape(owner_count, capacity, feature_width)
    full_basis = lax.all_gather(target_basis, "expert", axis=0, tiled=True)
    expert_part = run_expert(
        lax.all_to_all(outgoing, "expert", split_axis=0, concat_axis=0, tiled=True),
        gate_weight,
        up_weight,
        down_weight,
    )
    result = jnp.einsum("skd,dr->skr", expert_part, full_basis, preferred_element_type=jnp.float32)
    returned = lax.all_to_all(result, "expert", split_axis=0, concat_axis=0, tiled=True)
    summed = jnp.sum(returned.reshape(expert_count, SLICES, capacity, rank_width), axis=1)
    projected = summed.reshape(expert_count * capacity, rank_width)[slot_index]
    codes_float = gate_codes.astype(jnp.float32)
    weights = 2.5 * codes_float / jnp.sum(codes_float, axis=1, keepdims=True)
    projected = projected.reshape(token_count, pick_count, rank_width)
    return jnp.sum(weights[:, :, None] * projected, axis=1).astype(jnp.bfloat16)


def kernel(
    n, tok, ids, codes, gw, uw, dw, basis, out,
    wg, wu, wd, bs, x, accg, accu, ypart, yexch, yout, yrecv, zsend, zrecv,
    w_sem, b_sem, own_send, fwd_send, x_recv, e_send, e_recv, y_send, y_recv, z_send, z_recv,
):
    f32, bf16 = jnp.float32, jnp.bfloat16
    count, width = tok.shape
    parts = ROWS // count
    piece = width // parts
    chips = n // 2
    half = n * count // 2
    block = width // chips
    experts = n // SLICES
    me = lax.axis_index("expert")
    chip, core = me // 2, me % 2
    sib = chip * 2 + 1 - core
    my_half = me // chips

    def remote(src, dst, ssem, rsem, dev):
        return pltpu.make_async_remote_copy(
            src_ref=src, dst_ref=dst, send_sem=ssem, recv_sem=rsem,
            device_id={"expert": dev}, device_id_type=MESH,
        )

    loads = [
        pltpu.make_async_copy(src.at[0], dst, w_sem.at[i])
        for i, (src, dst) in enumerate(((gw, wg), (uw, wu), (dw, wd)))
    ]
    for load in loads:
        load.start()
    barrier = pltpu.get_barrier_semaphore()
    for k in range(1, n):
        pl.semaphore_signal(barrier, inc=1, device_id={"expert": (me + k) % n}, device_id_type=MESH)

    lane = lax.broadcasted_iota(jnp.int32, (count, LANES), 1)
    picked = codes[...].astype(f32)
    weights = 2.5 * picked / jnp.sum(picked, axis=1, keepdims=True)
    named = ids[...]
    both = jnp.zeros((count, LANES), f32)
    for k in range(named.shape[1]):
        e = named[:, k : k + 1]
        both += jnp.where((lane == e) | (lane == e + experts), weights[:, k : k + 1], 0.0)
    high = both.astype(bf16).astype(f32)
    extra = jnp.where(lane < experts, high, both - high)
    rows = tok[...].astype(f32)
    own = jnp.concatenate(
        [
            jnp.concatenate([rows[:, q * piece : (q + 1) * piece], extra], axis=1)
            for q in range(parts)
        ],
        axis=0,
    )
    x[me] = own.astype(bf16)
    pl.semaphore_wait(barrier, n - 1)

    sends = []
    for k in range(1, chips):
        c = remote(x.at[me], x.at[me], own_send.at[k], x_recv.at[me], ((chip + k) % chips) * 2 + core)
        c.start()
        sends.append(c)
    c = remote(x.at[me], x.at[me], fwd_send.at[0], x_recv.at[me], sib)
    c.start()
    sends.append(c)
    cb = remote(basis, bs.at[core], b_sem.at[0], b_sem.at[1], sib)
    cb.start()
    bs[core] = basis[...]
    for k in range(1, chips):
        src = ((chip + k) % chips) * 2 + core
        remote(x.at[src], x.at[src], own_send.at[0], x_recv.at[src], sib).wait_recv()
        c = remote(x.at[src], x.at[src], fwd_send.at[k], x_recv.at[src], sib)
        c.start()
        sends.append(c)
    for k in range(chips):
        src = ((chip + k) % chips) * 2 + 1 - core
        remote(x.at[src], x.at[src], own_send.at[0], x_recv.at[src], sib).wait_recv()
    loads[0].wait()
    loads[1].wait()

    total = n * ROWS
    place = lax.broadcasted_iota(jnp.int32, (total, 1), 0) % ROWS // count
    left = x[:, :, 0:piece].reshape(total, piece)

    def part(q, carry):
        at = pl.ds(pl.multiple_of(q * piece, LANES), piece)
        g = jnp.dot(left, wg[at, :], preferred_element_type=f32)
        accg[...] = jnp.where(place == q, g, accg[...])
        u = jnp.dot(left, wu[at, :], preferred_element_type=f32)
        accu[...] = jnp.where(place == q, u, accu[...])
        return carry

    accg[...] = jnp.zeros_like(accg)
    accu[...] = jnp.zeros_like(accu)
    lax.fori_loop(0, parts, part, 0)

    def fold(v):
        step = count
        while step < ROWS:
            v = v + pltpu.roll(v, total - step, 0)
            step *= 2
        return v

    g, u = fold(accg[...]), fold(accu[...])
    tail = x[:, :, piece:].reshape(total, LANES).astype(f32)
    lane = lax.broadcasted_iota(jnp.int32, (total, LANES), 1)
    mine = me // SLICES
    weight = jnp.sum(
        jnp.where((lane == mine) | (lane == mine + experts), tail, 0.0), axis=1, keepdims=True
    )
    hidden = (g / (1.0 + jnp.exp(-g)) * u * weight).astype(bf16)
    i = lax.broadcasted_iota(jnp.int32, (n * count, total), 0)
    j = lax.broadcasted_iota(jnp.int32, (n * count, total), 1)
    pick = jnp.where(j == i // count * ROWS + i % count, 1.0, 0.0).astype(bf16)
    hidden = jnp.dot(pick, hidden, preferred_element_type=f32).astype(bf16)

    loads[2].wait()
    for k in range(chips):
        to = (chip + 1 + k) % chips
        y = jnp.dot(
            hidden,
            wd[:, pl.ds(pl.multiple_of(to * block, LANES), block)],
            preferred_element_type=f32,
        ).astype(bf16)
        ypart[to] = y.reshape(2, half, block)
        c = remote(ypart.at[to, 1 - core], yexch.at[to], e_send.at[to], e_recv.at[to], sib)
        c.start()
        sends.append(c)
    for k in range(chips):
        to = (chip + 1 + k) % chips
        remote(yexch.at[to], yexch.at[to], e_send.at[to], e_recv.at[to], sib).wait_recv()
        summed = ypart[to, core].astype(f32) + yexch[to].astype(f32)
        if k == chips - 1:
            z = summed
        else:
            yout[to] = summed.astype(bf16)
            c = remote(yout.at[to], yrecv.at[chip], y_send.at[to], y_recv.at[chip], to * 2 + core)
            c.start()
            sends.append(c)
    for k in range(1, chips):
        src = (chip + chips - k) % chips
        remote(yrecv.at[src], yrecv.at[src], y_send.at[src], y_recv.at[src], sib).wait_recv()
        z = z + yrecv[src].astype(f32)

    cb.wait()
    full = bs[...].reshape(block, basis.shape[1])
    p = jnp.dot(z.astype(bf16), full, preferred_element_type=f32)
    for d in range(chips):
        zsend[d] = p[d * count : (d + 1) * count]
    for k in range(chips):
        d = (me + k) % chips
        c = remote(zsend.at[d], zrecv.at[chip], z_send.at[k], z_recv.at[chip], core * chips + d)
        if k == 0:

            @pl.when(my_half == core)
            def _():
                zrecv[chip] = zsend[d]

            @pl.when(my_half != core)
            def _():
                c.start()
                c.wait_send()
        else:
            c.start()
            sends.append(c)
    for src in range(chips):

        @pl.when(src * 2 + my_half != me)
        def _():
            remote(zrecv.at[src], zrecv.at[src], z_send.at[0], z_recv.at[src], sib).wait_recv()

    out[...] = jnp.sum(zrecv[...], axis=0).astype(bf16)
    for c in sends:
        c.wait_send()


def fused(tokens, expert_ids, gate_codes, gate_weight, up_weight, down_weight, target_basis):
    n = lax.axis_size("expert")
    count, width = tokens.shape
    unit = gate_weight.shape[2]
    rank = target_basis.shape[1]
    chips, half = n // 2, n * count // 2
    block = width // chips
    piece = width * count // ROWS
    bf16, f32 = jnp.bfloat16, jnp.float32
    dma = pltpu.SemaphoreType.DMA
    vmem = pl.BlockSpec(memory_space=pltpu.VMEM)
    hbm = pl.BlockSpec(memory_space=pl.ANY)
    return pl.pallas_call(
        functools.partial(kernel, n),
        out_shape=jax.ShapeDtypeStruct((count, rank), bf16),
        in_specs=[vmem, vmem, vmem, hbm, hbm, hbm, vmem],
        out_specs=vmem,
        scratch_shapes=[
            pltpu.VMEM((width, unit), bf16),
            pltpu.VMEM((width, unit), bf16),
            pltpu.VMEM((unit, width), bf16),
            pltpu.VMEM((2, width // n, rank), bf16),
            pltpu.VMEM((n, ROWS, piece + LANES), bf16),
            pltpu.VMEM((n * ROWS, unit), f32),
            pltpu.VMEM((n * ROWS, unit), f32),
            pltpu.VMEM((chips, 2, half, block), bf16),
            pltpu.VMEM((chips, half, block), bf16),
            pltpu.VMEM((chips, half, block), bf16),
            pltpu.VMEM((chips, half, block), bf16),
            pltpu.VMEM((chips, count, rank), f32),
            pltpu.VMEM((chips, count, rank), f32),
            dma((3,)),
            dma((2,)),
            dma((chips,)),
            dma((chips,)),
            dma((n,)),
            dma((chips,)),
            dma((chips,)),
            dma((chips,)),
            dma((chips,)),
            dma((chips,)),
            dma((chips,)),
        ],
        compiler_params=pltpu.CompilerParams(
            collective_id=0, has_side_effects=True, vmem_limit_bytes=40 * 2**20
        ),
    )(tokens, expert_ids, gate_codes, gate_weight, up_weight, down_weight, target_basis)


def shards(tokens, expert_ids, gate_codes, gate_weight, up_weight, down_weight, target_basis):
    n = lax.axis_size("expert")
    count, width = tokens.shape
    fits = (
        n % 2 == 0
        and ROWS % count == 0
        and width * count % (ROWS * LANES) == 0
        and (n * count) % (2 * ROWS) == 0
        and width % (n // 2 * LANES) == 0
        and width // n % ROWS == 0
        and 2 * (n // SLICES) <= LANES
    )
    run = fused if fits else gathered
    return run(
        tokens, expert_ids, gate_codes, gate_weight, up_weight, down_weight, target_basis
    )


def solution(mesh):
    in_specs = (
        P(("group", "expert"), None),
        P(("group", "expert"), None),
        P(("group", "expert"), None),
        P("expert", None, None),
        P("expert", None, None),
        P("expert", None, None),
        P("expert", None),
    )
    out_specs = P(("group", "expert"), None)
    return jax.shard_map(shards, mesh=mesh, in_specs=in_specs, out_specs=out_specs, check_vma=False)
```

```python
import functools

import jax
import jax.numpy as jnp
from jax import lax
from jax.experimental import pallas as pl
from jax.experimental.pallas import tpu as pltpu
from jax.sharding import PartitionSpec as P

SLICES = 8
LANES = 128
ROWS = 16
MESH = pl.DeviceIdType.MESH


def run_expert(received, gate_weight, up_weight, down_weight):
    sources, slots, feature_width = received.shape
    row_block = received.reshape(sources * slots, feature_width)
    gate_act = jnp.dot(row_block, gate_weight[0], preferred_element_type=jnp.float32)
    up_act = jnp.dot(row_block, up_weight[0], preferred_element_type=jnp.float32)
    hidden = (jax.nn.silu(gate_act) * up_act).astype(jnp.bfloat16)
    expert_part = jnp.dot(hidden, down_weight[0], preferred_element_type=jnp.float32).astype(
        jnp.bfloat16
    )
    return expert_part.reshape(sources, slots, feature_width)


def gathered(tokens, expert_ids, gate_codes, gate_weight, up_weight, down_weight, target_basis):
    token_count, feature_width = tokens.shape
    pick_count = expert_ids.shape[1]
    owner_count = lax.axis_size("expert")
    expert_count = owner_count // SLICES
    capacity = min(token_count, max(2, 5 * token_count * pick_count // (4 * expert_count)))
    rank_width = target_basis.shape[1]
    flat_ids = expert_ids.reshape(-1)
    order = jnp.arange(token_count * pick_count, dtype=jnp.int32)
    same = (flat_ids[:, None] == flat_ids[None, :]) & (order[None, :] < order[:, None])
    slot_rank = jnp.sum(same.astype(jnp.int32), axis=1)
    slot_index = flat_ids * capacity + slot_rank
    row_token = order // pick_count
    slot_table = (
        jnp.full((expert_count * capacity,), token_count, jnp.int32).at[slot_index].set(row_token)
    )
    padded = jnp.concatenate([tokens, jnp.zeros((1, feature_width), tokens.dtype)], axis=0)
    per_expert_rows = padded[slot_table].reshape(expert_count, 1, capacity, feature_width)
    outgoing = jnp.broadcast_to(per_expert_rows, (expert_count, SLICES, capacity, feature_width))
    outgoing = outgoing.reshape(owner_count, capacity, feature_width)
    full_basis = lax.all_gather(target_basis, "expert", axis=0, tiled=True)
    expert_part = run_expert(
        lax.all_to_all(outgoing, "expert", split_axis=0, concat_axis=0, tiled=True),
        gate_weight,
        up_weight,
        down_weight,
    )
    result = jnp.einsum("skd,dr->skr", expert_part, full_basis, preferred_element_type=jnp.float32)
    returned = lax.all_to_all(result, "expert", split_axis=0, concat_axis=0, tiled=True)
    summed = jnp.sum(returned.reshape(expert_count, SLICES, capacity, rank_width), axis=1)
    projected = summed.reshape(expert_count * capacity, rank_width)[slot_index]
    codes_float = gate_codes.astype(jnp.float32)
    weights = 2.5 * codes_float / jnp.sum(codes_float, axis=1, keepdims=True)
    projected = projected.reshape(token_count, pick_count, rank_width)
    return jnp.sum(weights[:, :, None] * projected, axis=1).astype(jnp.bfloat16)


def kernel(
    n, tok_in, ids, codes, gw, uw, dw, basis, out,
    tok, wg, wu, wd, bs, x, accg, accu, yown, ypart, yexch, yout, yrecv, zsend, zrecv,
    w_sem, b_sem, own_send, side_send, fwd_send, x_recv, e_send, e_recv, y_send, y_recv, z_send, z_recv,
):
    f32, bf16 = jnp.float32, jnp.bfloat16
    count, width = tok.shape
    parts = ROWS // count
    piece = width // parts
    chips = n // 2
    half = n * count // 2
    block = width // chips
    experts = n // SLICES
    me = lax.axis_index("expert")
    chip, core = me // 2, me % 2
    sib = chip * 2 + 1 - core
    across = 2 - chips % 2
    along = chips // across
    a, b = chip // across, chip % across

    def at(a, b, c):
        return (a % along * across + b % across) * 2 + c


    def remote(src, dst, ssem, rsem, dev):
        return pltpu.make_async_remote_copy(
            src_ref=src, dst_ref=dst, send_sem=ssem, recv_sem=rsem,
            device_id={"expert": dev}, device_id_type=MESH,
        )

    first = pltpu.make_async_copy(tok_in, tok, w_sem.at[3])
    first.start()
    loads = [
        pltpu.make_async_copy(src.at[0], dst, w_sem.at[i])
        for i, (src, dst) in enumerate(((gw, wg), (uw, wu), (dw, wd)))
    ]
    barrier = pltpu.get_barrier_semaphore()
    for peer in [sib] + [((chip + k) % chips) * 2 + core for k in range(1, chips)]:
        pl.semaphore_signal(barrier, inc=1, device_id={"expert": peer}, device_id_type=MESH)

    for load in loads:
        load.start()
    mb = pltpu.make_async_copy(basis, bs.at[core], b_sem.at[2])
    mb.start()
    lane = lax.broadcasted_iota(jnp.int32, (count, LANES), 1)
    picked = codes[...].astype(f32)
    weights = 2.5 * picked / jnp.sum(picked, axis=0, keepdims=True)
    named = ids[...].astype(f32)
    square = (count, count)
    diagonal = lax.broadcasted_iota(jnp.int32, square, 0) == lax.broadcasted_iota(
        jnp.int32, square, 1
    )

    def column(row):
        return jnp.sum(
            jnp.where(diagonal, jnp.broadcast_to(row, square), 0.0), axis=1, keepdims=True
        )

    both = jnp.zeros((count, LANES), f32)
    for k in range(named.shape[0]):
        e = column(named[k : k + 1])
        spot = lane.astype(f32)
        both += jnp.where((spot == e) | (spot == e + experts), column(weights[k : k + 1]), 0.0)
    high = both.astype(bf16).astype(f32)
    extra = jnp.where(lane < experts, high, both - high)
    first.wait()
    rows = tok[...].astype(f32)
    own = jnp.concatenate(
        [
            jnp.concatenate([rows[:, q * piece : (q + 1) * piece], extra], axis=1)
            for q in range(parts)
        ],
        axis=0,
    )
    x[me] = own.astype(bf16)
    pl.semaphore_wait(barrier, chips)

    sends = []

    def pass_on(src, sem, dev):
        c = remote(x.at[src], x.at[src], sem, x_recv.at[src], dev)
        c.start()
        sends.append(c)

    def arrived(src):
        remote(x.at[src], x.at[src], own_send.at[0], x_recv.at[src], sib).wait_recv()

    steps = [k for k in (1, along - 1) if 0 < k < along]
    steps = list(dict.fromkeys(steps + list(range(1, along))))
    for k in steps:
        pass_on(me, own_send.at[k], at(a + k, b, core))
    if across == 2:
        pass_on(me, side_send.at[0], at(a, b + 1, core))
    pass_on(me, fwd_send.at[0], sib)
    for k in steps:
        src = at(a + along - k, b, core)
        arrived(src)
        if across == 2:
            pass_on(src, side_send.at[k], at(a, b + 1, core))
        pass_on(src, fwd_send.at[k], sib)
    if across == 2:
        for k in [0] + steps:
            src = at(a + along - k, b + 1, core)
            arrived(src)
            pass_on(src, fwd_send.at[along + k], sib)
    cb = remote(basis, bs.at[core], b_sem.at[0], b_sem.at[1], sib)
    cb.start()
    for k in range(chips):
        arrived(((chip + k) % chips) * 2 + 1 - core)
    loads[0].wait()
    loads[1].wait()

    total = n * ROWS
    place = lax.broadcasted_iota(jnp.int32, (total, 1), 0) % ROWS // count
    left = x[:, :, 0:piece].reshape(total, piece)

    def part(q, carry):
        span = pl.ds(pl.multiple_of(q * piece, LANES), piece)
        g = jnp.dot(left, wg[span, :], preferred_element_type=f32)
        accg[...] = jnp.where(place == q, g, accg[...])
        u = jnp.dot(left, wu[span, :], preferred_element_type=f32)
        accu[...] = jnp.where(place == q, u, accu[...])
        return carry

    accg[...] = jnp.zeros_like(accg)
    accu[...] = jnp.zeros_like(accu)
    lax.fori_loop(0, parts, part, 0)

    def fold(v):
        step = count
        while step < ROWS:
            v = v + pltpu.roll(v, total - step, 0)
            step *= 2
        return v

    g, u = fold(accg[...]), fold(accu[...])
    hidden = (g / (1.0 + jnp.exp(-g)) * u).astype(bf16)
    i = lax.broadcasted_iota(jnp.int32, (n * count, total), 0)
    owner = i % half // count * 2 + (i // half + core) % 2
    j = lax.broadcasted_iota(jnp.int32, (n * count, total), 1)
    pick = jnp.where(j == owner * ROWS + i % count, 1.0, 0.0).astype(bf16)
    hidden = jnp.dot(pick, hidden, preferred_element_type=f32).astype(bf16)
    tail = x[:, :, piece:].reshape(total, LANES)
    tail = jnp.dot(pick, tail, preferred_element_type=f32)
    lane = lax.broadcasted_iota(jnp.int32, (n * count, LANES), 1)
    mine = me // SLICES
    weight = jnp.sum(
        jnp.where((lane == mine) | (lane == mine + experts), tail, 0.0), axis=1, keepdims=True
    )

    loads[2].wait()
    z = None
    lag = 2
    for k in range(chips + lag):
        if k < chips:
            to = (chip + 1 + k) % chips
            y = jnp.dot(
                hidden,
                wd[:, pl.ds(pl.multiple_of(to * block, LANES), block)],
                preferred_element_type=f32,
            )
            y = y * weight
            ypart[to] = y[half:].astype(bf16)
            c = remote(ypart.at[to], yexch.at[to], e_send.at[to], e_recv.at[to], sib)
            c.start()
            sends.append(c)
            yown[to] = y[:half]
        if k >= lag:
            to = (chip + 1 + k - lag) % chips
            remote(yexch.at[to], yexch.at[to], e_send.at[to], e_recv.at[to], sib).wait_recv()
            summed = yown[to] + yexch[to].astype(f32)
            if k - lag == chips - 1:
                z = summed
            else:
                yout[to] = summed.astype(bf16)
                c = remote(
                    yout.at[to], yrecv.at[chip], y_send.at[to], y_recv.at[chip], to * 2 + core
                )
                c.start()
                sends.append(c)
    for k in range(1, chips):
        src = (chip + chips - k) % chips
        remote(yrecv.at[src], yrecv.at[src], y_send.at[src], y_recv.at[src], sib).wait_recv()
        z = z + yrecv[src].astype(f32)

    cb.wait()
    mb.wait()
    full = bs[...].reshape(block, basis.shape[1])
    coarse = z.astype(bf16)
    fine = (z - coarse.astype(f32)).astype(bf16)
    p = jnp.dot(jnp.concatenate([coarse, fine], axis=0), full, preferred_element_type=f32)
    p = p[:half] + p[half:]
    for d in range(chips):
        zsend[d] = p[d * count : (d + 1) * count]
    for k in range(1, chips):
        d = (chip + k) % chips
        c = remote(zsend.at[d], zrecv.at[chip], z_send.at[k], z_recv.at[chip], d * 2 + core)
        c.start()
        sends.append(c)
    zrecv[chip] = zsend[chip]
    for k in range(1, chips):
        src = (chip + chips - k) % chips
        remote(zrecv.at[src], zrecv.at[src], z_send.at[0], z_recv.at[src], sib).wait_recv()

    out[...] = jnp.sum(zrecv[...], axis=0).astype(bf16)
    for c in sends:
        c.wait_send()


def fused(tokens, expert_ids, gate_codes, gate_weight, up_weight, down_weight, target_basis):
    n = lax.axis_size("expert")
    count, width = tokens.shape
    unit = gate_weight.shape[2]
    rank = target_basis.shape[1]
    chips, half = n // 2, n * count // 2
    block = width // chips
    piece = width * count // ROWS
    bf16, f32 = jnp.bfloat16, jnp.float32
    dma = pltpu.SemaphoreType.DMA
    vmem = pl.BlockSpec(memory_space=pltpu.VMEM)
    hbm = pl.BlockSpec(memory_space=pltpu.HBM)
    return pl.pallas_call(
        functools.partial(kernel, n),
        out_shape=jax.ShapeDtypeStruct((count, rank), bf16),
        in_specs=[hbm, vmem, vmem, hbm, hbm, hbm, hbm],
        out_specs=vmem,
        scratch_shapes=[
            pltpu.VMEM((count, width), bf16),
            pltpu.VMEM((width, unit), bf16),
            pltpu.VMEM((width, unit), bf16),
            pltpu.VMEM((unit, width), bf16),
            pltpu.VMEM((2, width // n, rank), bf16),
            pltpu.VMEM((n, ROWS, piece + LANES), bf16),
            pltpu.VMEM((n * ROWS, unit), f32),
            pltpu.VMEM((n * ROWS, unit), f32),
            pltpu.VMEM((chips, half, block), f32),
            pltpu.VMEM((chips, half, block), bf16),
            pltpu.VMEM((chips, half, block), bf16),
            pltpu.VMEM((chips, half, block), bf16),
            pltpu.VMEM((chips, half, block), bf16),
            pltpu.VMEM((chips, count, rank), f32),
            pltpu.VMEM((chips, count, rank), f32),
            dma((4,)),
            dma((3,)),
            dma((chips,)),
            dma((chips,)),
            dma((chips,)),
            dma((n,)),
            dma((chips,)),
            dma((chips,)),
            dma((chips,)),
            dma((chips,)),
            dma((chips,)),
            dma((chips,)),
        ],
        compiler_params=pltpu.CompilerParams(
            collective_id=0, has_side_effects=True, vmem_limit_bytes=60 * 2**20
        ),
    )(tokens, expert_ids.T, gate_codes.T, gate_weight, up_weight, down_weight, target_basis)


def shards(tokens, expert_ids, gate_codes, gate_weight, up_weight, down_weight, target_basis):
    n = lax.axis_size("expert")
    count, width = tokens.shape
    fits = (
        n % 2 == 0
        and ROWS % count == 0
        and width * count % (ROWS * LANES) == 0
        and (n * count) % (2 * ROWS) == 0
        and width % (n // 2 * LANES) == 0
        and width // n % ROWS == 0
        and 2 * (n // SLICES) <= LANES
    )
    run = fused if fits else gathered
    return run(
        tokens, expert_ids, gate_codes, gate_weight, up_weight, down_weight, target_basis
    )


def solution(mesh):
    in_specs = (
        P(("group", "expert"), None),
        P(("group", "expert"), None),
        P(("group", "expert"), None),
        P("expert", None, None),
        P("expert", None, None),
        P("expert", None, None),
        P("expert", None),
    )
    out_specs = P(("group", "expert"), None)
    return jax.shard_map(shards, mesh=mesh, in_specs=in_specs, out_specs=out_specs, check_vma=False)
```

```python
import functools

import jax
import jax.numpy as jnp
from jax import lax
from jax.experimental import pallas as pl
from jax.experimental.pallas import tpu as pltpu
from jax.sharding import PartitionSpec as P

SLICES = 8
LANES = 128
ROWS = 16
MESH = pl.DeviceIdType.MESH


def run_expert(received, gate_weight, up_weight, down_weight):
    sources, slots, feature_width = received.shape
    row_block = received.reshape(sources * slots, feature_width)
    gate_act = jnp.dot(row_block, gate_weight[0], preferred_element_type=jnp.float32)
    up_act = jnp.dot(row_block, up_weight[0], preferred_element_type=jnp.float32)
    hidden = (jax.nn.silu(gate_act) * up_act).astype(jnp.bfloat16)
    expert_part = jnp.dot(hidden, down_weight[0], preferred_element_type=jnp.float32).astype(
        jnp.bfloat16
    )
    return expert_part.reshape(sources, slots, feature_width)


def gathered(tokens, expert_ids, gate_codes, gate_weight, up_weight, down_weight, target_basis):
    token_count, feature_width = tokens.shape
    pick_count = expert_ids.shape[1]
    owner_count = lax.axis_size("expert")
    expert_count = owner_count // SLICES
    capacity = min(token_count, max(2, 5 * token_count * pick_count // (4 * expert_count)))
    rank_width = target_basis.shape[1]
    flat_ids = expert_ids.reshape(-1)
    order = jnp.arange(token_count * pick_count, dtype=jnp.int32)
    same = (flat_ids[:, None] == flat_ids[None, :]) & (order[None, :] < order[:, None])
    slot_rank = jnp.sum(same.astype(jnp.int32), axis=1)
    slot_index = flat_ids * capacity + slot_rank
    row_token = order // pick_count
    slot_table = (
        jnp.full((expert_count * capacity,), token_count, jnp.int32).at[slot_index].set(row_token)
    )
    padded = jnp.concatenate([tokens, jnp.zeros((1, feature_width), tokens.dtype)], axis=0)
    per_expert_rows = padded[slot_table].reshape(expert_count, 1, capacity, feature_width)
    outgoing = jnp.broadcast_to(per_expert_rows, (expert_count, SLICES, capacity, feature_width))
    outgoing = outgoing.reshape(owner_count, capacity, feature_width)
    full_basis = lax.all_gather(target_basis, "expert", axis=0, tiled=True)
    expert_part = run_expert(
        lax.all_to_all(outgoing, "expert", split_axis=0, concat_axis=0, tiled=True),
        gate_weight,
        up_weight,
        down_weight,
    )
    result = jnp.einsum("skd,dr->skr", expert_part, full_basis, preferred_element_type=jnp.float32)
    returned = lax.all_to_all(result, "expert", split_axis=0, concat_axis=0, tiled=True)
    summed = jnp.sum(returned.reshape(expert_count, SLICES, capacity, rank_width), axis=1)
    projected = summed.reshape(expert_count * capacity, rank_width)[slot_index]
    codes_float = gate_codes.astype(jnp.float32)
    weights = 2.5 * codes_float / jnp.sum(codes_float, axis=1, keepdims=True)
    projected = projected.reshape(token_count, pick_count, rank_width)
    return jnp.sum(weights[:, :, None] * projected, axis=1).astype(jnp.bfloat16)


def kernel(
    n, tok_in, ids, codes, gw, uw, dw, basis, out,
    tok, wg, wu, wd, bs, x, accg, accu, yown, ypart, yexch, yout, yside, yrecv, zsend, zrecv,
    w_sem, b_sem, own_send, side_send, fwd_send, x_recv, e_send, e_recv, y_send, s_recv, y_recv, z_send, z_recv,
):
    f32, bf16 = jnp.float32, jnp.bfloat16
    count, width = tok.shape
    parts = ROWS // count
    piece = width // parts
    chips = n // 2
    half = n * count // 2
    block = width // chips
    experts = n // SLICES
    me = lax.axis_index("expert")
    chip, core = me // 2, me % 2
    sib = chip * 2 + 1 - core
    across = 2 - chips % 2
    along = chips // across
    a, b = chip // across, chip % across

    def at(a, b, c):
        return (a % along * across + b % across) * 2 + c


    def remote(src, dst, ssem, rsem, dev):
        return pltpu.make_async_remote_copy(
            src_ref=src, dst_ref=dst, send_sem=ssem, recv_sem=rsem,
            device_id={"expert": dev}, device_id_type=MESH,
        )

    first = pltpu.make_async_copy(tok_in, tok, w_sem.at[3])
    first.start()
    loads = [
        pltpu.make_async_copy(src.at[0], dst, w_sem.at[i])
        for i, (src, dst) in enumerate(((gw, wg), (uw, wu), (dw, wd)))
    ]
    barrier = pltpu.get_barrier_semaphore()
    for peer in [sib] + [((chip + k) % chips) * 2 + core for k in range(1, chips)]:
        pl.semaphore_signal(barrier, inc=1, device_id={"expert": peer}, device_id_type=MESH)

    for load in loads:
        load.start()
    mb = pltpu.make_async_copy(basis, bs.at[core], b_sem.at[2])
    mb.start()
    lane = lax.broadcasted_iota(jnp.int32, (count, LANES), 1)
    picked = codes[...].astype(f32)
    weights = 2.5 * picked / jnp.sum(picked, axis=0, keepdims=True)
    named = ids[...].astype(f32)
    square = (count, count)
    diagonal = lax.broadcasted_iota(jnp.int32, square, 0) == lax.broadcasted_iota(
        jnp.int32, square, 1
    )

    def column(row):
        return jnp.sum(
            jnp.where(diagonal, jnp.broadcast_to(row, square), 0.0), axis=1, keepdims=True
        )

    both = jnp.zeros((count, LANES), f32)
    for k in range(named.shape[0]):
        e = column(named[k : k + 1])
        spot = lane.astype(f32)
        both += jnp.where((spot == e) | (spot == e + experts), column(weights[k : k + 1]), 0.0)
    high = both.astype(bf16).astype(f32)
    extra = jnp.where(lane < experts, high, both - high)
    first.wait()
    rows = tok[...].astype(f32)
    own = jnp.concatenate(
        [
            jnp.concatenate([rows[:, q * piece : (q + 1) * piece], extra], axis=1)
            for q in range(parts)
        ],
        axis=0,
    )
    x[me] = own.astype(bf16)
    pl.semaphore_wait(barrier, chips)

    sends = []

    def pass_on(src, sem, dev):
        c = remote(x.at[src], x.at[src], sem, x_recv.at[src], dev)
        c.start()
        sends.append(c)

    def arrived(src):
        remote(x.at[src], x.at[src], own_send.at[0], x_recv.at[src], sib).wait_recv()

    steps = [k for k in (1, along - 1) if 0 < k < along]
    steps = list(dict.fromkeys(steps + list(range(1, along))))
    for k in steps:
        pass_on(me, own_send.at[k], at(a + k, b, core))
    if across == 2:
        pass_on(me, side_send.at[0], at(a, b + 1, core))
    pass_on(me, fwd_send.at[0], sib)
    for k in steps:
        src = at(a + along - k, b, core)
        arrived(src)
        if across == 2:
            pass_on(src, side_send.at[k], at(a, b + 1, core))
        pass_on(src, fwd_send.at[k], sib)
    if across == 2:
        for k in [0] + steps:
            src = at(a + along - k, b + 1, core)
            arrived(src)
            pass_on(src, fwd_send.at[along + k], sib)
    cb = remote(basis, bs.at[core], b_sem.at[0], b_sem.at[1], sib)
    cb.start()
    for k in range(chips):
        arrived(((chip + k) % chips) * 2 + 1 - core)
    loads[0].wait()
    loads[1].wait()

    total = n * ROWS
    place = lax.broadcasted_iota(jnp.int32, (total, 1), 0) % ROWS // count
    left = x[:, :, 0:piece].reshape(total, piece)

    def part(q, carry):
        span = pl.ds(pl.multiple_of(q * piece, LANES), piece)
        g = jnp.dot(left, wg[span, :], preferred_element_type=f32)
        accg[...] = jnp.where(place == q, g, accg[...])
        u = jnp.dot(left, wu[span, :], preferred_element_type=f32)
        accu[...] = jnp.where(place == q, u, accu[...])
        return carry

    accg[...] = jnp.zeros_like(accg)
    accu[...] = jnp.zeros_like(accu)
    lax.fori_loop(0, parts, part, 0)

    def fold(v):
        step = count
        while step < ROWS:
            v = v + pltpu.roll(v, total - step, 0)
            step *= 2
        return v

    g, u = fold(accg[...]), fold(accu[...])
    hidden = (g / (1.0 + jnp.exp(-g)) * u).astype(bf16)
    i = lax.broadcasted_iota(jnp.int32, (n * count, total), 0)
    owner = i % half // count * 2 + (i // half + core) % 2
    j = lax.broadcasted_iota(jnp.int32, (n * count, total), 1)
    pick = jnp.where(j == owner * ROWS + i % count, 1.0, 0.0).astype(bf16)
    hidden = jnp.dot(pick, hidden, preferred_element_type=f32).astype(bf16)
    tail = x[:, :, piece:].reshape(total, LANES)
    tail = jnp.dot(pick, tail, preferred_element_type=f32)
    lane = lax.broadcasted_iota(jnp.int32, (n * count, LANES), 1)
    mine = me // SLICES
    weight = jnp.sum(
        jnp.where((lane == mine) | (lane == mine + experts), tail, 0.0), axis=1, keepdims=True
    )

    loads[2].wait()
    order = steps + [0]
    turns = [(k, d) for d in range(across - 1, -1, -1) for k in order]
    lag = 2
    for t in range(chips + lag):
        if t < chips:
            to = at(a + turns[t][0], b + turns[t][1], 0) // 2
            y = jnp.dot(
                hidden,
                wd[:, pl.ds(pl.multiple_of(to * block, LANES), block)],
                preferred_element_type=f32,
            )
            y = y * weight
            ypart[to] = y[half:].astype(bf16)
            c = remote(ypart.at[to], yexch.at[to], e_send.at[to], e_recv.at[to], sib)
            c.start()
            sends.append(c)
            yown[to] = y[:half]
        if t >= lag:
            k, d = turns[t - lag]
            to = at(a + k, b + d, 0) // 2
            remote(yexch.at[to], yexch.at[to], e_send.at[to], e_recv.at[to], sib).wait_recv()
            summed = yown[to] + yexch[to].astype(f32)
            if d == 0:
                yown[to] = summed
            else:
                yout[to] = summed.astype(bf16)
                slot = (a + k) % along
                c = remote(
                    yout.at[to], yside.at[slot], y_send.at[to], s_recv.at[slot], at(a, b + 1, core)
                )
                c.start()
                sends.append(c)
    for k in order:
        slot = (a + k) % along
        to = at(a + k, b, 0) // 2
        z = yown[to]
        if across == 2:
            remote(
                yside.at[slot], yside.at[slot], y_send.at[to], s_recv.at[slot], sib
            ).wait_recv()
            z = z + yside[slot].astype(f32)
        if k:
            yout[to] = z.astype(bf16)
            c = remote(yout.at[to], yrecv.at[a], y_send.at[to], y_recv.at[a], at(a + k, b, core))
            c.start()
            sends.append(c)
    for k in steps:
        src = (a + along - k) % along
        remote(yrecv.at[src], yrecv.at[src], y_send.at[src], y_recv.at[src], sib).wait_recv()
        z = z + yrecv[src].astype(f32)

    cb.wait()
    mb.wait()
    full = bs[...].reshape(block, basis.shape[1])
    coarse = z.astype(bf16)
    fine = (z - coarse.astype(f32)).astype(bf16)
    p = jnp.dot(jnp.concatenate([coarse, fine], axis=0), full, preferred_element_type=f32)
    p = p[:half] + p[half:]
    for d in range(chips):
        zsend[d] = p[d * count : (d + 1) * count]
    for k in range(1, chips):
        d = (chip + k) % chips
        c = remote(zsend.at[d], zrecv.at[chip], z_send.at[k], z_recv.at[chip], d * 2 + core)
        c.start()
        sends.append(c)
    zrecv[chip] = zsend[chip]
    for k in range(1, chips):
        src = (chip + chips - k) % chips
        remote(zrecv.at[src], zrecv.at[src], z_send.at[0], z_recv.at[src], sib).wait_recv()

    out[...] = jnp.sum(zrecv[...], axis=0).astype(bf16)
    for c in sends:
        c.wait_send()


def fused(tokens, expert_ids, gate_codes, gate_weight, up_weight, down_weight, target_basis):
    n = lax.axis_size("expert")
    count, width = tokens.shape
    unit = gate_weight.shape[2]
    rank = target_basis.shape[1]
    chips, half = n // 2, n * count // 2
    block = width // chips
    piece = width * count // ROWS
    bf16, f32 = jnp.bfloat16, jnp.float32
    dma = pltpu.SemaphoreType.DMA
    vmem = pl.BlockSpec(memory_space=pltpu.VMEM)
    hbm = pl.BlockSpec(memory_space=pltpu.HBM)
    return pl.pallas_call(
        functools.partial(kernel, n),
        out_shape=jax.ShapeDtypeStruct((count, rank), bf16),
        in_specs=[hbm, vmem, vmem, hbm, hbm, hbm, hbm],
        out_specs=vmem,
        scratch_shapes=[
            pltpu.VMEM((count, width), bf16),
            pltpu.VMEM((width, unit), bf16),
            pltpu.VMEM((width, unit), bf16),
            pltpu.VMEM((unit, width), bf16),
            pltpu.VMEM((2, width // n, rank), bf16),
            pltpu.VMEM((n, ROWS, piece + LANES), bf16),
            pltpu.VMEM((n * ROWS, unit), f32),
            pltpu.VMEM((n * ROWS, unit), f32),
            pltpu.VMEM((chips, half, block), f32),
            pltpu.VMEM((chips, half, block), bf16),
            pltpu.VMEM((chips, half, block), bf16),
            pltpu.VMEM((chips, half, block), bf16),
            pltpu.VMEM((chips, half, block), bf16),
            pltpu.VMEM((chips, half, block), bf16),
            pltpu.VMEM((chips, count, rank), f32),
            pltpu.VMEM((chips, count, rank), f32),
            dma((4,)),
            dma((3,)),
            dma((chips,)),
            dma((chips,)),
            dma((chips,)),
            dma((n,)),
            dma((chips,)),
            dma((chips,)),
            dma((chips,)),
            dma((chips,)),
            dma((chips,)),
            dma((chips,)),
            dma((chips,)),
        ],
        compiler_params=pltpu.CompilerParams(
            collective_id=0, has_side_effects=True, vmem_limit_bytes=60 * 2**20
        ),
    )(tokens, expert_ids.T, gate_codes.T, gate_weight, up_weight, down_weight, target_basis)


def shards(tokens, expert_ids, gate_codes, gate_weight, up_weight, down_weight, target_basis):
    n = lax.axis_size("expert")
    count, width = tokens.shape
    fits = (
        n % 2 == 0
        and ROWS % count == 0
        and width * count % (ROWS * LANES) == 0
        and (n * count) % (2 * ROWS) == 0
        and width % (n // 2 * LANES) == 0
        and width // n % ROWS == 0
        and 2 * (n // SLICES) <= LANES
    )
    run = fused if fits else gathered
    return run(
        tokens, expert_ids, gate_codes, gate_weight, up_weight, down_weight, target_basis
    )


def solution(mesh):
    in_specs = (
        P(("group", "expert"), None),
        P(("group", "expert"), None),
        P(("group", "expert"), None),
        P("expert", None, None),
        P("expert", None, None),
        P("expert", None, None),
        P("expert", None),
    )
    out_specs = P(("group", "expert"), None)
    return jax.shard_map(shards, mesh=mesh, in_specs=in_specs, out_specs=out_specs, check_vma=False)
```

```python
import functools

import jax
import jax.numpy as jnp
from jax import lax
from jax.experimental import pallas as pl
from jax.experimental.pallas import tpu as pltpu
from jax.sharding import PartitionSpec as P

SLICES = 8
LANES = 128
ROWS = 16
MESH = pl.DeviceIdType.MESH


def run_expert(received, gate_weight, up_weight, down_weight):
    sources, slots, feature_width = received.shape
    row_block = received.reshape(sources * slots, feature_width)
    gate_act = jnp.dot(row_block, gate_weight[0], preferred_element_type=jnp.float32)
    up_act = jnp.dot(row_block, up_weight[0], preferred_element_type=jnp.float32)
    hidden = (jax.nn.silu(gate_act) * up_act).astype(jnp.bfloat16)
    expert_part = jnp.dot(hidden, down_weight[0], preferred_element_type=jnp.float32).astype(
        jnp.bfloat16
    )
    return expert_part.reshape(sources, slots, feature_width)


def gathered(tokens, expert_ids, gate_codes, gate_weight, up_weight, down_weight, target_basis):
    token_count, feature_width = tokens.shape
    pick_count = expert_ids.shape[1]
    owner_count = lax.axis_size("expert")
    expert_count = owner_count // SLICES
    capacity = min(token_count, max(2, 5 * token_count * pick_count // (4 * expert_count)))
    rank_width = target_basis.shape[1]
    flat_ids = expert_ids.reshape(-1)
    order = jnp.arange(token_count * pick_count, dtype=jnp.int32)
    same = (flat_ids[:, None] == flat_ids[None, :]) & (order[None, :] < order[:, None])
    slot_rank = jnp.sum(same.astype(jnp.int32), axis=1)
    slot_index = flat_ids * capacity + slot_rank
    row_token = order // pick_count
    slot_table = (
        jnp.full((expert_count * capacity,), token_count, jnp.int32).at[slot_index].set(row_token)
    )
    padded = jnp.concatenate([tokens, jnp.zeros((1, feature_width), tokens.dtype)], axis=0)
    per_expert_rows = padded[slot_table].reshape(expert_count, 1, capacity, feature_width)
    outgoing = jnp.broadcast_to(per_expert_rows, (expert_count, SLICES, capacity, feature_width))
    outgoing = outgoing.reshape(owner_count, capacity, feature_width)
    full_basis = lax.all_gather(target_basis, "expert", axis=0, tiled=True)
    expert_part = run_expert(
        lax.all_to_all(outgoing, "expert", split_axis=0, concat_axis=0, tiled=True),
        gate_weight,
        up_weight,
        down_weight,
    )
    result = jnp.einsum("skd,dr->skr", expert_part, full_basis, preferred_element_type=jnp.float32)
    returned = lax.all_to_all(result, "expert", split_axis=0, concat_axis=0, tiled=True)
    summed = jnp.sum(returned.reshape(expert_count, SLICES, capacity, rank_width), axis=1)
    projected = summed.reshape(expert_count * capacity, rank_width)[slot_index]
    codes_float = gate_codes.astype(jnp.float32)
    weights = 2.5 * codes_float / jnp.sum(codes_float, axis=1, keepdims=True)
    projected = projected.reshape(token_count, pick_count, rank_width)
    return jnp.sum(weights[:, :, None] * projected, axis=1).astype(jnp.bfloat16)


def kernel(
    n, tok_in, ids, codes, gw, uw, dw, basis, out,
    tok, wg, wu, wd, bs, x, accg, accu, yown, ypart, yexch, yout, yside, yrecv, zsend, zrecv,
    w_sem, b_sem, own_send, side_send, fwd_send, x_recv, e_send, e_recv, y_send, s_recv, y_recv, z_send, z_recv,
):
    f32, bf16 = jnp.float32, jnp.bfloat16
    count, width = tok.shape
    parts = ROWS // count
    piece = width // parts
    chips = n // 2
    half = n * count // 2
    block = width // chips
    experts = n // SLICES
    me = lax.axis_index("expert")
    chip, core = me // 2, me % 2
    sib = chip * 2 + 1 - core
    across = 2 - chips % 2
    along = chips // across
    a, b = chip // across, chip % across

    def at(a, b, c):
        return (a % along * across + b % across) * 2 + c


    def place_of(dev):
        owner = dev // 2
        return (owner % across * along + owner // across) * 2 + dev % 2

    def remote(src, dst, ssem, rsem, dev):
        return pltpu.make_async_remote_copy(
            src_ref=src, dst_ref=dst, send_sem=ssem, recv_sem=rsem,
            device_id={"expert": dev}, device_id_type=MESH,
        )

    first = pltpu.make_async_copy(tok_in, tok, w_sem.at[3])
    first.start()
    loads = [
        pltpu.make_async_copy(src.at[0], dst, w_sem.at[i])
        for i, (src, dst) in enumerate(((gw, wg), (uw, wu), (dw, wd)))
    ]
    barrier = pltpu.get_barrier_semaphore()
    for peer in [sib] + [((chip + k) % chips) * 2 + core for k in range(1, chips)]:
        pl.semaphore_signal(barrier, inc=1, device_id={"expert": peer}, device_id_type=MESH)

    for load in loads:
        load.start()
    mb = pltpu.make_async_copy(basis, bs.at[core], b_sem.at[2])
    mb.start()
    lane = lax.broadcasted_iota(jnp.int32, (count, LANES), 1)
    picked = codes[...].astype(f32)
    weights = 2.5 * picked / jnp.sum(picked, axis=0, keepdims=True)
    named = ids[...].astype(f32)
    square = (count, count)
    diagonal = lax.broadcasted_iota(jnp.int32, square, 0) == lax.broadcasted_iota(
        jnp.int32, square, 1
    )

    def column(row):
        return jnp.sum(
            jnp.where(diagonal, jnp.broadcast_to(row, square), 0.0), axis=1, keepdims=True
        )

    both = jnp.zeros((count, LANES), f32)
    for k in range(named.shape[0]):
        e = column(named[k : k + 1])
        spot = lane.astype(f32)
        both += jnp.where((spot == e) | (spot == e + experts), column(weights[k : k + 1]), 0.0)
    high = both.astype(bf16).astype(f32)
    extra = jnp.where(lane < experts, high, both - high)
    first.wait()
    rows = tok[...].astype(f32)
    own = jnp.concatenate(
        [
            jnp.concatenate([rows[:, q * piece : (q + 1) * piece], extra], axis=1)
            for q in range(parts)
        ],
        axis=0,
    )
    x[place_of(me)] = own.astype(bf16)
    pl.semaphore_wait(barrier, chips)

    sends = []

    def pass_on(src, sem, dev):
        slot = place_of(src)
        c = remote(x.at[slot], x.at[slot], sem, x_recv.at[slot], dev)
        c.start()
        sends.append(c)

    def arrived(src):
        slot = place_of(src)
        remote(x.at[slot], x.at[slot], own_send.at[0], x_recv.at[slot], sib).wait_recv()

    lines = along * 2 * ROWS
    place = lax.broadcasted_iota(jnp.int32, (lines, 1), 0) % ROWS // count

    def part(q, col):
        left = x[pl.ds(col * (along * 2), along * 2), :, 0:piece].reshape(lines, piece)
        to = pl.ds(pl.multiple_of(col * lines, ROWS), lines)
        for w, acc in ((wg, accg), (wu, accu)):
            v = jnp.dot(left, w[q * piece : (q + 1) * piece, :], preferred_element_type=f32)
            acc[to, :] = v if q == 0 else jnp.where(place == q, v, acc[to, :])

    steps = [k for k in (1, along - 1) if 0 < k < along]
    steps = list(dict.fromkeys(steps + list(range(1, along))))
    for k in steps:
        pass_on(me, own_send.at[k], at(a + k, b, core))
    if across == 2:
        pass_on(me, side_send.at[0], at(a, b + 1, core))
    pass_on(me, fwd_send.at[0], sib)
    for k in steps:
        src = at(a + along - k, b, core)
        arrived(src)
        if across == 2:
            pass_on(src, side_send.at[k], at(a, b + 1, core))
        pass_on(src, fwd_send.at[k], sib)
    cb = remote(basis, bs.at[core], b_sem.at[0], b_sem.at[1], sib)
    cb.start()
    for k in [0] + steps:
        arrived(at(a + along - k, b, 1 - core))
    loads[0].wait()
    loads[1].wait()
    others = [at(a + along - k, b + 1, core) for k in [0] + steps] if across == 2 else []
    for q in range(max(parts, len(others))):
        if q < parts:
            part(q, b)
        if q < len(others):
            arrived(others[q])
            pass_on(others[q], fwd_send.at[along + q], sib)
    if across == 2:
        for k in [0] + steps:
            arrived(at(a + along - k, b + 1, 1 - core))
        for q in range(parts):
            part(q, 1 - b)

    total = n * ROWS

    def fold(v):
        step = count
        while step < ROWS:
            v = v + pltpu.roll(v, total - step, 0)
            step *= 2
        return v

    g, u = fold(accg[...]), fold(accu[...])
    hidden = (g / (1.0 + jnp.exp(-g)) * u).astype(bf16)
    i = lax.broadcasted_iota(jnp.int32, (n * count, total), 0)
    owner = i % half // count * 2 + (i // half + core) % 2
    j = lax.broadcasted_iota(jnp.int32, (n * count, total), 1)
    pick = jnp.where(j == place_of(owner) * ROWS + i % count, 1.0, 0.0).astype(bf16)
    hidden = jnp.dot(pick, hidden, preferred_element_type=f32).astype(bf16)
    tail = x[:, :, piece:].reshape(total, LANES)
    tail = jnp.dot(pick, tail, preferred_element_type=f32)
    lane = lax.broadcasted_iota(jnp.int32, (n * count, LANES), 1)
    mine = me // SLICES
    weight = jnp.sum(
        jnp.where((lane == mine) | (lane == mine + experts), tail, 0.0), axis=1, keepdims=True
    )

    loads[2].wait()
    order = steps + [0]
    turns = [(k, d) for d in range(across - 1, -1, -1) for k in order]
    lag = 2
    for t in range(chips + lag):
        if t < chips:
            to = at(a + turns[t][0], b + turns[t][1], 0) // 2
            y = jnp.dot(
                hidden,
                wd[:, pl.ds(pl.multiple_of(to * block, LANES), block)],
                preferred_element_type=f32,
            )
            y = y * weight
            ypart[to] = y[half:].astype(bf16)
            c = remote(ypart.at[to], yexch.at[to], e_send.at[to], e_recv.at[to], sib)
            c.start()
            sends.append(c)
            yown[to] = y[:half]
        if t >= lag:
            k, d = turns[t - lag]
            to = at(a + k, b + d, 0) // 2
            remote(yexch.at[to], yexch.at[to], e_send.at[to], e_recv.at[to], sib).wait_recv()
            summed = yown[to] + yexch[to].astype(f32)
            if d == 0:
                yown[to] = summed
            else:
                yout[to] = summed.astype(bf16)
                slot = (a + k) % along
                c = remote(
                    yout.at[to], yside.at[slot], y_send.at[to], s_recv.at[slot], at(a, b + 1, core)
                )
                c.start()
                sends.append(c)
    for k in order:
        slot = (a + k) % along
        to = at(a + k, b, 0) // 2
        z = yown[to]
        if across == 2:
            remote(
                yside.at[slot], yside.at[slot], y_send.at[to], s_recv.at[slot], sib
            ).wait_recv()
            z = z + yside[slot].astype(f32)
        if k:
            yout[to] = z.astype(bf16)
            c = remote(yout.at[to], yrecv.at[a], y_send.at[to], y_recv.at[a], at(a + k, b, core))
            c.start()
            sends.append(c)
    for k in steps:
        src = (a + along - k) % along
        remote(yrecv.at[src], yrecv.at[src], y_send.at[src], y_recv.at[src], sib).wait_recv()
        z = z + yrecv[src].astype(f32)

    cb.wait()
    mb.wait()
    full = bs[...].reshape(block, basis.shape[1])
    coarse = z.astype(bf16)
    fine = (z - coarse.astype(f32)).astype(bf16)
    p = jnp.dot(jnp.concatenate([coarse, fine], axis=0), full, preferred_element_type=f32)
    p = p[:half] + p[half:]
    for d in range(chips):
        zsend[d] = p[d * count : (d + 1) * count]
    for k in range(1, chips):
        d = (chip + k) % chips
        c = remote(zsend.at[d], zrecv.at[chip], z_send.at[k], z_recv.at[chip], d * 2 + core)
        c.start()
        sends.append(c)
    zrecv[chip] = zsend[chip]
    for k in range(1, chips):
        src = (chip + chips - k) % chips
        remote(zrecv.at[src], zrecv.at[src], z_send.at[0], z_recv.at[src], sib).wait_recv()

    out[...] = jnp.sum(zrecv[...], axis=0).astype(bf16)
    for c in sends:
        c.wait_send()


def fused(tokens, expert_ids, gate_codes, gate_weight, up_weight, down_weight, target_basis):
    n = lax.axis_size("expert")
    count, width = tokens.shape
    unit = gate_weight.shape[2]
    rank = target_basis.shape[1]
    chips, half = n // 2, n * count // 2
    block = width // chips
    piece = width * count // ROWS
    bf16, f32 = jnp.bfloat16, jnp.float32
    dma = pltpu.SemaphoreType.DMA
    vmem = pl.BlockSpec(memory_space=pltpu.VMEM)
    hbm = pl.BlockSpec(memory_space=pltpu.HBM)
    return pl.pallas_call(
        functools.partial(kernel, n),
        out_shape=jax.ShapeDtypeStruct((count, rank), bf16),
        in_specs=[hbm, vmem, vmem, hbm, hbm, hbm, hbm],
        out_specs=vmem,
        scratch_shapes=[
            pltpu.VMEM((count, width), bf16),
            pltpu.VMEM((width, unit), bf16),
            pltpu.VMEM((width, unit), bf16),
            pltpu.VMEM((unit, width), bf16),
            pltpu.VMEM((2, width // n, rank), bf16),
            pltpu.VMEM((n, ROWS, piece + LANES), bf16),
            pltpu.VMEM((n * ROWS, unit), f32),
            pltpu.VMEM((n * ROWS, unit), f32),
            pltpu.VMEM((chips, half, block), f32),
            pltpu.VMEM((chips, half, block), bf16),
            pltpu.VMEM((chips, half, block), bf16),
            pltpu.VMEM((chips, half, block), bf16),
            pltpu.VMEM((chips, half, block), bf16),
            pltpu.VMEM((chips, half, block), bf16),
            pltpu.VMEM((chips, count, rank), f32),
            pltpu.VMEM((chips, count, rank), f32),
            dma((4,)),
            dma((3,)),
            dma((chips,)),
            dma((chips,)),
            dma((chips,)),
            dma((n,)),
            dma((chips,)),
            dma((chips,)),
            dma((chips,)),
            dma((chips,)),
            dma((chips,)),
            dma((chips,)),
            dma((chips,)),
        ],
        compiler_params=pltpu.CompilerParams(
            collective_id=0, has_side_effects=True, vmem_limit_bytes=60 * 2**20
        ),
    )(tokens, expert_ids.T, gate_codes.T, gate_weight, up_weight, down_weight, target_basis)


def shards(tokens, expert_ids, gate_codes, gate_weight, up_weight, down_weight, target_basis):
    n = lax.axis_size("expert")
    count, width = tokens.shape
    fits = (
        n % 2 == 0
        and ROWS % count == 0
        and width * count % (ROWS * LANES) == 0
        and (n * count) % (2 * ROWS) == 0
        and width % (n // 2 * LANES) == 0
        and width // n % ROWS == 0
        and 2 * (n // SLICES) <= LANES
    )
    run = fused if fits else gathered
    return run(
        tokens, expert_ids, gate_codes, gate_weight, up_weight, down_weight, target_basis
    )


def solution(mesh):
    in_specs = (
        P(("group", "expert"), None),
        P(("group", "expert"), None),
        P(("group", "expert"), None),
        P("expert", None, None),
        P("expert", None, None),
        P("expert", None, None),
        P("expert", None),
    )
    out_specs = P(("group", "expert"), None)
    return jax.shard_map(shards, mesh=mesh, in_specs=in_specs, out_specs=out_specs, check_vma=False)
```
